32 devices in a mesh: lat: 4 (over x, core), lon: 8 (over z, y).
Axes of the slice: x: 2, y: 2, z: 4, core: 2. Of those that a mesh axis runs over, the one named last changes fastest.
Arguments:
- vorticity: float32 [16, 2, 256, 8192], P(None, None, 'lat', 'lon'), may hold values from -6 to 6
- legendre: bfloat16 [2048, 2048, 256], P(('lat', 'lon')), may hold values from -0.25 to 0.25
- wave_order: int32 [2048], replicated, may hold values from 0 to 2047, each once
Outputs:
- spectral: float32 [2048, 2, 16, 2048], P(('lat', 'lon'))
The draws below stay inside these ranges and needn't reach their ends.
Inputs may be any that keep to these rules, and one draw needn't show every extreme that they name: wave_order is a permutation: every wavenumber below 2048 is held by exactly one slot.
All inputs are finite; a program needn't handle non-finite values.
Results may differ from the reference program's by a relative error of at most 0.0029.
Values may be sent and summed in bfloat16 or wider, within the bound.
No kernel may reach another device: no remote copies, remote signals or barrier semaphores. Data moves between devices by JAX's collectives and lax.ppermute only.
A program may use at most 192 MiB of HBM per device.

```python
import math
import jax
import jax.numpy as jnp
from jax import lax

NLON = 8192
MW = 2048
LEV = 16
LATH = 256
NDEG = 2048


def levels(key, shape, cuts, least, largest):
    factor_of, own = 1.0, jax.random.fold_in(key, 6)
    for dim, blocks in cuts:
        heights = jnp.exp(jax.random.uniform(jax.random.fold_in(own, dim), (blocks,), jnp.float32, least / len(cuts), largest / len(cuts)))
        factor_of = factor_of * jnp.repeat(heights, shape[dim] // blocks).reshape([-1 if axis == dim else 1 for axis in range(len(shape))])
    return factor_of


def bell_draw(key, dims, spread, reach, cuts=(), kind=jnp.bfloat16):
    factor_of = levels(key, dims, cuts, -0.22, 0.18) if cuts else 1.0
    drawn = jax.random.normal(key, dims, jnp.float32) * spread * factor_of
    return jnp.minimum(jnp.maximum(drawn, -reach), reach).astype(kind)


def setup_inputs(seed: int = 0) -> dict:
    arg_keys = jax.random.split(jax.random.key(seed), 4)
    vorticity = bell_draw(arg_keys[0], (LEV, 2, LATH, NLON), 1.0, 6.0, ((2, 4), (3, 8)), jnp.float32)
    legendre = bell_draw(arg_keys[1], (MW, NDEG, LATH), (2 * LATH) ** -0.5, 0.25, ((0, 32),))
    wave_order = jax.random.permutation(arg_keys[2], MW).astype(jnp.int32)
    return dict(vorticity=vorticity, legendre=legendre, wave_order=wave_order)


def reference(vorticity, legendre, wave_order):
    coefficient = jnp.fft.rfft(vorticity, axis=-1)[..., :MW] / math.sqrt(NLON)
    fourier = jnp.stack([jnp.real(coefficient), jnp.imag(coefficient)], axis=3).astype(jnp.bfloat16)
    chosen = jnp.take(fourier, wave_order, axis=4)
    per_slot = jnp.transpose(chosen, (4, 2, 1, 3, 0)).reshape(MW, LATH, 4 * LEV)
    degree = jnp.arange(NDEG, dtype=jnp.int32)
    parity = (1 - 2 * (degree % 2)).astype(jnp.float32)

    def one_slot(packed):
        table, column_data, wave = packed
        product = jnp.dot(column_data.T, table.T, preferred_element_type=jnp.float32)
        product = product.reshape(2, 2, LEV, NDEG)
        combined = product[0] + parity * product[1]
        return jnp.where(degree < MW - wave, combined, jnp.zeros_like(combined))
    return lax.map(one_slot, (legendre, per_slot, wave_order))
```

```python
import functools
import math

import jax
import jax.numpy as jnp
import numpy as np
from jax import lax
from jax.experimental import pallas as pl
from jax.experimental.pallas import tpu as pltpu
from jax.sharding import PartitionSpec as P

MW = 2048
FIRST = 64
LANES = 128
KEEP = MW // FIRST
HALF = FIRST // 2 + 1
ROWS_K = 4 * KEEP
KTILE = 256
PRESCALE = 8192.0
VMEM = 56 * 1024 * 1024


def second_tables(circle):
    b = np.arange(LANES)[None, :]
    scale = 1.0 / math.sqrt(circle) / PRESCALE
    table = np.zeros((HALF, 2, KEEP, 2, 2 * LANES), np.float64)
    for k in range(HALF):
        for side in range(2):
            first = k if side == 0 else FIRST - k
            m = (first + FIRST * np.arange(KEEP))[:, None]
            angle = 2.0 * np.pi / circle * ((m * b) % circle)
            c, s = np.cos(angle), np.sin(angle)
            sign = 1.0 if side == 0 else -1.0
            table[k, side, :, 0, :LANES] = c
            table[k, side, :, 0, LANES:] = sign * s
            table[k, side, :, 1, :LANES] = -s
            table[k, side, :, 1, LANES:] = sign * c
    table = (table * scale).astype(np.float32).reshape(HALF, ROWS_K, 2 * LANES)
    high = table.astype(jnp.bfloat16)
    low = (table - high.astype(np.float32)).astype(jnp.bfloat16)
    return high, low


def add(a, b):
    return (a[0] + b[0], a[1] + b[1])


def sub(a, b):
    return (a[0] - b[0], a[1] - b[1])


def minus_i(a):
    return (a[1], -a[0])


def times(a, angle):
    c, s = math.cos(angle), math.sin(angle)
    return (a[0] * c + a[1] * s, a[1] * c - a[0] * s)


def real_dft8(x):
    r = math.sqrt(0.5)
    s04, d04 = x[0] + x[4], x[0] - x[4]
    s26, d26 = x[2] + x[6], x[2] - x[6]
    s15, d15 = x[1] + x[5], x[1] - x[5]
    s37, d37 = x[3] + x[7], x[3] - x[7]
    even, odd = s04 + s26, s15 + s37
    p, q = r * (d15 - d37), r * (d15 + d37)
    return [
        (even + odd, None),
        (d04 + p, -(d26 + q)),
        (s04 - s26, -(s15 - s37)),
        (d04 - p, d26 - q),
        (even - odd, None),
    ]


def complex_dft8(x):
    r = math.sqrt(0.5)

    def dft4(a, b, c, d):
        s, t, u, v = add(a, c), sub(a, c), add(b, d), minus_i(sub(b, d))
        return [add(s, u), add(t, v), sub(s, u), sub(t, v)]

    even = dft4(x[0], x[2], x[4], x[6])
    odd = dft4(x[1], x[3], x[5], x[7])
    o1 = ((odd[1][0] + odd[1][1]) * r, (odd[1][1] - odd[1][0]) * r)
    o2 = minus_i(odd[2])
    o3 = ((odd[3][1] - odd[3][0]) * r, -(odd[3][0] + odd[3][1]) * r)
    turned = [odd[0], o1, o2, o3]
    return [add(e, o) for e, o in zip(even, turned)] + [sub(e, o) for e, o in zip(even, turned)]


def fourier_kernel(rows, slots, index_ref, x_ref, high_ref, low_ref, out_ref, stage, y_high, y_low, full, picked):
    per_source = x_ref.shape[2] // LANES
    group = 16

    def put(k, row, value):
        for part in range(2):
            at = (k, pl.ds(row, group), pl.ds(part * LANES, LANES))
            v = value[part]
            if v is None:
                v = jnp.zeros((group, LANES), jnp.float32)
            h = v.astype(jnp.bfloat16)
            y_high[at] = h
            y_low[at] = (v - h.astype(jnp.float32)).astype(jnp.bfloat16)

    def first_step(step, carry):
        row = pl.multiple_of(step * group, group)
        for t in range(8):
            x = []
            for s in range(8):
                source, piece = divmod(8 * s + t, per_source)
                x.append(x_ref[source, pl.ds(row, group), pl.ds(piece * LANES, LANES)])
            for k1, (real, imag) in enumerate(real_dft8(x)):
                stage[t, k1, 0] = real
                if imag is not None:
                    stage[t, k1, 1] = imag
        for k2, value in enumerate(real_dft8([stage[t, 0, 0] for t in range(8)])):
            put(8 * k2, row, value)
        for k1 in range(1, 5):
            turned = []
            for t in range(8):
                angle = 2.0 * math.pi * t * k1 / FIRST
                if k1 == 4:
                    real = stage[t, k1, 0]
                    turned.append((real * math.cos(angle), real * -math.sin(angle)))
                else:
                    turned.append(times((stage[t, k1, 0], stage[t, k1, 1]), angle))
            for k2, value in enumerate(complex_dft8(turned)):
                k = k1 + 8 * k2
                if k < HALF:
                    put(k, row, value)
                elif k1 != 4:
                    put(FIRST - k, row, (value[0], -value[1]))
        return carry

    lax.fori_loop(0, rows // group, first_step, 0)

    def dot(a, b):
        return lax.dot_general(a, b, (((1,), (1,)), ((), ())), preferred_element_type=jnp.float32)

    def second_step(k, carry):
        at = pl.ds(pl.multiple_of(k * ROWS_K, ROWS_K), ROWS_K)
        full[at, :] = dot(high_ref[k], y_high[k]) + (dot(high_ref[k], y_low[k]) + dot(low_ref[k], y_high[k]))
        return carry

    lax.fori_loop(0, HALF, second_step, 0)

    def pick(step, carry):
        first = step * 8
        for i in range(8):
            at = pl.multiple_of(index_ref[first + i], 2)
            to = pl.multiple_of(step * 16, 16) + 2 * i
            picked[pl.ds(to, 2), :] = full[pl.ds(at, 2), :]
        return carry

    lax.fori_loop(0, slots // 8, pick, 0)
    out_ref[...] = picked[...].astype(jnp.bfloat16)


def fourier_slots(x, index, high, low):
    sources, rows, part = x.shape
    slots = index.shape[0]
    return pl.pallas_call(
        functools.partial(fourier_kernel, rows, slots),
        out_shape=jax.ShapeDtypeStruct((slots * 2, rows), jnp.bfloat16),
        in_specs=[pl.BlockSpec(memory_space=pltpu.SMEM)] + [pl.BlockSpec(memory_space=pltpu.VMEM)] * 3,
        out_specs=pl.BlockSpec(memory_space=pltpu.VMEM),
        scratch_shapes=[
            pltpu.VMEM((8, 5, 2, 16, LANES), jnp.float32),
            pltpu.VMEM((HALF, rows, 2 * LANES), jnp.bfloat16),
            pltpu.VMEM((HALF, rows, 2 * LANES), jnp.bfloat16),
            pltpu.VMEM((HALF * ROWS_K, rows), jnp.float32),
            pltpu.VMEM((slots * 2, rows), jnp.float32),
        ],
        compiler_params=pltpu.CompilerParams(vmem_limit_bytes=VMEM),
        cost_estimate=pl.CostEstimate(
            flops=6 * HALF * ROWS_K * rows * 2 * LANES, bytes_accessed=12 * 1024 * 1024, transcendentals=0
        ),
        name="fourier_slots",
    )(index, x, high, low)


def legendre_kernel(slots, tiles, buffers, limit_ref, data_ref, table_ref, out_ref, held, sems):
    slot = pl.program_id(0)
    degrees = tiles * KTILE

    def copy(s, tile):
        rows = pl.ds(tile * KTILE, KTILE)
        place = lax.rem(s, buffers)
        return pltpu.make_async_copy(table_ref.at[s, rows, :], held.at[place, rows, :], sems.at[place, tile])

    def start(s):
        for tile in range(tiles):

            @pl.when(tile * KTILE < limit_ref[s])
            def _():
                copy(s, tile).start()

    @pl.when(slot == 0)
    def _():
        for s in range(min(buffers - 1, slots)):
            start(s)

    @pl.when(slot + buffers - 1 < slots)
    def _():
        start(slot + buffers - 1)

    limit = limit_ref[slot]
    place = lax.rem(slot, buffers)
    data = data_ref[0]
    half = data.shape[0] // 2
    shape = out_ref.shape[1:3] + (KTILE,)
    degree = lax.broadcasted_iota(jnp.int32, (half, KTILE), 1)
    parity = (1 - 2 * (degree % 2)).astype(jnp.float32)
    for tile in range(tiles):
        cols = pl.ds(tile * KTILE, KTILE)

        @pl.when(tile * KTILE < limit)
        def _():
            copy(slot, tile).wait()
            product = lax.dot_general(
                data, held[place, cols, :], (((1,), (1,)), ((), ())), preferred_element_type=jnp.float32
            )
            both = product[:half] + parity * product[half:]
            both = jnp.where(degree < limit - tile * KTILE, both, 0.0)
            out_ref[0, :, :, cols] = both.reshape(shape)

        @pl.when(tile * KTILE >= limit)
        def _():
            out_ref[0, :, :, cols] = jnp.zeros(shape, jnp.float32)


def legendre_sum(limits, data, table, levels):
    slots, degrees, lats = table.shape
    columns = data.shape[1]
    tiles = degrees // KTILE
    buffers = 6
    return pl.pallas_call(
        functools.partial(legendre_kernel, slots, tiles, buffers),
        grid_spec=pltpu.PrefetchScalarGridSpec(
            num_scalar_prefetch=1,
            grid=(slots,),
            in_specs=[
                pl.BlockSpec((1, columns, lats), lambda s, lim: (s, 0, 0)),
                pl.BlockSpec(memory_space=pl.ANY),
            ],
            out_specs=pl.BlockSpec((1, 2, levels, degrees), lambda s, lim: (s, 0, 0, 0)),
            scratch_shapes=[
                pltpu.VMEM((buffers, degrees, lats), jnp.bfloat16),
                pltpu.SemaphoreType.DMA((buffers, tiles)),
            ],
        ),
        out_shape=jax.ShapeDtypeStruct((slots, 2, levels, degrees), jnp.float32),
        compiler_params=pltpu.CompilerParams(vmem_limit_bytes=VMEM),
        cost_estimate=pl.CostEstimate(
            flops=slots * degrees * lats * columns, bytes_accessed=slots * degrees * (lats + 64 * 2), transcendentals=0
        ),
        name="legendre_sum",
    )(limits, data, table)


def on_device(lat_size, lon_size, high, low, vorticity, legendre, wave_order):
    levels, hemis, lats, part = vorticity.shape
    slot_count = legendre.shape[0]
    waves = wave_order.astype(jnp.int32)
    lower, upper = waves % FIRST, waves // FIRST
    near = lower < HALF
    index = jnp.where(near, lower, FIRST - lower) * ROWS_K + jnp.where(near, 0, 2 * KEEP) + 2 * upper
    first_slot = lax.axis_index(("lat", "lon")) * slot_count
    limits = waves.shape[0] - lax.dynamic_slice_in_dim(waves, first_slot, slot_count)
    chunks = levels // lon_size
    pieces = []
    for chunk in range(chunks):
        block = vorticity[chunk * lon_size : (chunk + 1) * lon_size] * PRESCALE
        block = block.astype(jnp.float16).reshape(lon_size, hemis * lats, part)
        block = lax.all_to_all(block, "lon", split_axis=0, concat_axis=0, tiled=True)
        chosen = fourier_slots(block.astype(jnp.float32), index, high, low)
        chosen = chosen.reshape(lat_size * lon_size, slot_count * 2, hemis * lats)
        moved = lax.all_to_all(chosen, ("lat", "lon"), split_axis=0, concat_axis=0, tiled=True)
        moved = moved.reshape(lat_size, lon_size, slot_count, 2, hemis, lats)
        pieces.append(moved)
    data = jnp.stack(pieces, axis=0)
    data = jnp.transpose(data, (3, 5, 4, 0, 2, 1, 6)).reshape(slot_count, hemis * 2 * levels, lat_size * lats)
    return legendre_sum(limits, data, legendre, levels)


def solution(mesh):
    lat_size, lon_size = mesh.shape["lat"], mesh.shape["lon"]

    def whole(vorticity, legendre, wave_order):
        high, low = second_tables(vorticity.shape[3])
        body = functools.partial(on_device, lat_size, lon_size, high, low)
        return jax.shard_map(
            body,
            mesh=mesh,
            in_specs=(P(None, None, "lat", "lon"), P(("lat", "lon"), None, None), P()),
            out_specs=P(("lat", "lon"), None, None, None),
            check_vma=False,
        )(vorticity, legendre, wave_order)

    return whole
```

```python
import functools
import math

import jax
import jax.numpy as jnp
import numpy as np
from jax import lax
from jax.experimental import pallas as pl
from jax.experimental.pallas import tpu as pltpu
from jax.sharding import PartitionSpec as P

MW = 2048
FIRST = 64
LANES = 128
KEEP = MW // FIRST
HALF = FIRST // 2 + 1
ROWS_K = 4 * KEEP
KTILE = 256
PRESCALE = 8192.0
VMEM = 56 * 1024 * 1024


def second_tables(circle):
    b = np.arange(LANES)[None, :]
    scale = 1.0 / math.sqrt(circle) / PRESCALE
    table = np.zeros((HALF, 2, KEEP, 2, 2 * LANES), np.float64)
    for k in range(HALF):
        for side in range(2):
            first = k if side == 0 else FIRST - k
            m = (first + FIRST * np.arange(KEEP))[:, None]
            angle = 2.0 * np.pi / circle * ((m * b) % circle)
            c, s = np.cos(angle), np.sin(angle)
            sign = 1.0 if side == 0 else -1.0
            table[k, side, :, 0, :LANES] = c
            table[k, side, :, 0, LANES:] = sign * s
            table[k, side, :, 1, :LANES] = -s
            table[k, side, :, 1, LANES:] = sign * c
    table = (table * scale).astype(np.float32).reshape(HALF, ROWS_K, 2 * LANES)
    high = table.astype(jnp.bfloat16)
    low = (table - high.astype(np.float32)).astype(jnp.bfloat16)
    return high, low


def add(a, b):
    return (a[0] + b[0], a[1] + b[1])


def sub(a, b):
    return (a[0] - b[0], a[1] - b[1])


def minus_i(a):
    return (a[1], -a[0])


def times(a, angle):
    c, s = math.cos(angle), math.sin(angle)
    return (a[0] * c + a[1] * s, a[1] * c - a[0] * s)


def real_dft8(x):
    r = math.sqrt(0.5)
    s04, d04 = x[0] + x[4], x[0] - x[4]
    s26, d26 = x[2] + x[6], x[2] - x[6]
    s15, d15 = x[1] + x[5], x[1] - x[5]
    s37, d37 = x[3] + x[7], x[3] - x[7]
    even, odd = s04 + s26, s15 + s37
    p, q = r * (d15 - d37), r * (d15 + d37)
    return [
        (even + odd, None),
        (d04 + p, -(d26 + q)),
        (s04 - s26, -(s15 - s37)),
        (d04 - p, d26 - q),
        (even - odd, None),
    ]


def complex_dft8(x):
    r = math.sqrt(0.5)

    def dft4(a, b, c, d):
        s, t, u, v = add(a, c), sub(a, c), add(b, d), minus_i(sub(b, d))
        return [add(s, u), add(t, v), sub(s, u), sub(t, v)]

    even = dft4(x[0], x[2], x[4], x[6])
    odd = dft4(x[1], x[3], x[5], x[7])
    o1 = ((odd[1][0] + odd[1][1]) * r, (odd[1][1] - odd[1][0]) * r)
    o2 = minus_i(odd[2])
    o3 = ((odd[3][1] - odd[3][0]) * r, -(odd[3][0] + odd[3][1]) * r)
    turned = [odd[0], o1, o2, o3]
    return [add(e, o) for e, o in zip(even, turned)] + [sub(e, o) for e, o in zip(even, turned)]


def fourier_kernel(rows, slots, parts, index_ref, me_ref, x_ref, high_ref, low_ref, *refs):
    out_refs = refs[:parts]
    stage, y_high, y_low, full, picked = refs[parts:]
    me = me_ref[0]
    per_source = x_ref.shape[2] // LANES
    group = 16

    def put(k, row, value):
        for part in range(2):
            at = (k, pl.ds(row, group), pl.ds(part * LANES, LANES))
            v = value[part]
            if v is None:
                v = jnp.zeros((group, LANES), jnp.float32)
            h = v.astype(jnp.bfloat16)
            y_high[at] = h
            y_low[at] = (v - h.astype(jnp.float32)).astype(jnp.bfloat16)

    def first_step(step, carry):
        row = pl.multiple_of(step * group, group)
        for t in range(8):
            x = []
            for s in range(8):
                source, piece = divmod(8 * s + t, per_source)
                x.append(x_ref[me ^ source, pl.ds(row, group), pl.ds(piece * LANES, LANES)])
            for k1, (real, imag) in enumerate(real_dft8(x)):
                stage[t, k1, 0] = real
                if imag is not None:
                    stage[t, k1, 1] = imag
        for k2, value in enumerate(real_dft8([stage[t, 0, 0] for t in range(8)])):
            put(8 * k2, row, value)
        for k1 in range(1, 5):
            turned = []
            for t in range(8):
                angle = 2.0 * math.pi * t * k1 / FIRST
                if k1 == 4:
                    real = stage[t, k1, 0]
                    turned.append((real * math.cos(angle), real * -math.sin(angle)))
                else:
                    turned.append(times((stage[t, k1, 0], stage[t, k1, 1]), angle))
            for k2, value in enumerate(complex_dft8(turned)):
                k = k1 + 8 * k2
                if k < HALF:
                    put(k, row, value)
                elif k1 != 4:
                    put(FIRST - k, row, (value[0], -value[1]))
        return carry

    lax.fori_loop(0, rows // group, first_step, 0)

    def dot(a, b):
        return lax.dot_general(a, b, (((1,), (1,)), ((), ())), preferred_element_type=jnp.float32)

    def second_step(k, carry):
        at = pl.ds(pl.multiple_of(k * ROWS_K, ROWS_K), ROWS_K)
        full[at, :] = dot(high_ref[k], y_high[k]) + (dot(high_ref[k], y_low[k]) + dot(low_ref[k], y_high[k]))
        return carry

    lax.fori_loop(0, HALF, second_step, 0)

    def pick(step, carry):
        first = step * 8
        for i in range(8):
            at = pl.multiple_of(index_ref[first + i], 2)
            to = pl.multiple_of(step * 16, 16) + 2 * i
            picked[pl.ds(to, 2), :] = full[pl.ds(at, 2), :]
        return carry

    lax.fori_loop(0, slots // 8, pick, 0)
    length = slots * 2 // parts
    for part in range(parts):
        out_refs[part][...] = picked[pl.ds(part * length, length), :].astype(jnp.bfloat16)


def fourier_slots(x, me, index, high, low, parts):
    sources, rows, part = x.shape
    slots = index.shape[0]
    smem, vmem = pl.BlockSpec(memory_space=pltpu.SMEM), pl.BlockSpec(memory_space=pltpu.VMEM)
    return pl.pallas_call(
        functools.partial(fourier_kernel, rows, slots, parts),
        out_shape=[jax.ShapeDtypeStruct((slots * 2 // parts, rows), jnp.bfloat16)] * parts,
        in_specs=[smem, smem, vmem, vmem, vmem],
        out_specs=[vmem] * parts,
        scratch_shapes=[
            pltpu.VMEM((8, 5, 2, 16, LANES), jnp.float32),
            pltpu.VMEM((HALF, rows, 2 * LANES), jnp.bfloat16),
            pltpu.VMEM((HALF, rows, 2 * LANES), jnp.bfloat16),
            pltpu.VMEM((HALF * ROWS_K, rows), jnp.float32),
            pltpu.VMEM((slots * 2, rows), jnp.float32),
        ],
        compiler_params=pltpu.CompilerParams(vmem_limit_bytes=VMEM),
        cost_estimate=pl.CostEstimate(
            flops=6 * HALF * ROWS_K * rows * 2 * LANES, bytes_accessed=12 * 1024 * 1024, transcendentals=0
        ),
        name="fourier_slots",
    )(index, me, x, high, low)


def arrange_kernel(lat_size, lon_size, slots, moved_ref, out_ref, sorted_rows):
    rows = slots * 2
    for lat in range(lat_size):
        for lon in range(lon_size):
            block = moved_ref[lat * lon_size + lon].astype(jnp.float32)
            sorted_rows[lat, pl.ds(lon, rows, stride=lon_size), :] = block
    shape = (slots, 2 * lon_size, LANES)
    lane = lax.broadcasted_iota(jnp.int32, (rows * lon_size, LANES), 1)
    lower = lane < LANES // 2
    for pair in range(lat_size // 2):
        first, second = sorted_rows[2 * pair], sorted_rows[2 * pair + 1]
        north = jnp.where(lower, first, pltpu.roll(second, LANES // 2, 1))
        south = jnp.where(lower, pltpu.roll(first, LANES // 2, 1), second)
        lanes = pl.ds(pair * LANES, LANES)
        out_ref[:, 0, :, lanes] = north.reshape(shape).astype(jnp.bfloat16)
        out_ref[:, 1, :, lanes] = south.reshape(shape).astype(jnp.bfloat16)


def arrange(moved, lat_size, lon_size, slots):
    rows = moved.shape[2]
    lats = rows // 2
    if rows != LANES or lon_size != 8:
        moved = moved.reshape(lat_size, lon_size, slots, 2, 2, lats)
        moved = jnp.transpose(moved, (2, 4, 3, 1, 0, 5))
        return moved.reshape(slots, 2, 2 * lon_size, lat_size * lats)
    return pl.pallas_call(
        functools.partial(arrange_kernel, lat_size, lon_size, slots),
        out_shape=jax.ShapeDtypeStruct((slots, 2, 2 * lon_size, lat_size * lats), jnp.bfloat16),
        in_specs=[pl.BlockSpec(memory_space=pltpu.VMEM)],
        out_specs=pl.BlockSpec(memory_space=pltpu.VMEM),
        scratch_shapes=[pltpu.VMEM((lat_size, slots * 2 * lon_size, LANES), jnp.float32)],
        compiler_params=pltpu.CompilerParams(vmem_limit_bytes=VMEM),
        cost_estimate=pl.CostEstimate(flops=1024, bytes_accessed=16 * 1024 * 1024, transcendentals=0),
        name="arrange",
    )(moved)


def legendre_kernel(begin, end, tiles, bases, first, *refs):
    limit_ref, refs = refs[0], refs[1:]
    data_refs, refs = refs[: len(bases)], refs[len(bases) :]
    table_ref, refs = refs[0], refs[1 if first else 2 :]
    out_ref, held, staged, in_sems, out_sems = refs
    buffers, stages = held.shape[0], staged.shape[0]
    levels = out_ref.shape[2]
    part = levels // len(bases)
    half = 2 * levels

    def tile_count(slot):
        return lax.div(limit_ref[slot] + (KTILE - 1), KTILE)

    def fetch(slot, count):
        place = lax.rem(slot, buffers)
        rows = pl.ds(0, count * KTILE)
        return pltpu.make_async_copy(table_ref.at[slot, rows, :], held.at[place, rows, :], in_sems.at[place])

    def put(slot):
        place = lax.rem(slot, stages)
        return pltpu.make_async_copy(staged.at[place], out_ref.at[slot], out_sems.at[place])

    def start(slot):
        count = tile_count(slot)
        for n in range(1, tiles + 1):

            @pl.when(count == n)
            def _():
                fetch(slot, n).start()

    ahead = min(buffers - 1, end - begin)
    for i in range(ahead):
        start(begin + i)
    degree = lax.broadcasted_iota(jnp.int32, (half, KTILE), 1)
    parity = (1 - 2 * (degree % 2)).astype(jnp.float32)

    def one(slot, carry):
        @pl.when(slot + ahead < end)
        def _():
            start(slot + ahead)

        limit = limit_ref[slot]
        place, stage = lax.rem(slot, buffers), lax.rem(slot, stages)
        count = tile_count(slot)
        pieces = [ref[slot - base, h] for h in range(2) for ref, base in zip(data_refs, bases)]
        data = jnp.concatenate(pieces, axis=0)

        @pl.when(slot - begin >= stages)
        def _():
            put(slot - stages).wait()

        for n in range(1, tiles + 1):

            @pl.when(count == n)
            def _():
                fetch(slot, n).wait()
                product = lax.dot_general(
                    data,
                    held[place, 0 : n * KTILE, :],
                    (((1,), (1,)), ((), ())),
                    preferred_element_type=jnp.float32,
                )
                for t in range(n):
                    cols = slice(t * KTILE, (t + 1) * KTILE)
                    both = product[:half, cols] + parity * product[half:, cols]
                    if t == n - 1:
                        both = jnp.where(degree < limit - t * KTILE, both, 0.0)
                    for chunk in range(len(bases)):
                        for c in range(2):
                            at = (chunk * 2 + c) * part
                            staged[stage, c, chunk * part : (chunk + 1) * part, cols] = both[at : at + part]
                if n < tiles:
                    rest = (tiles - n) * KTILE
                    staged[stage, :, :, n * KTILE :] = jnp.zeros((2, levels, rest), jnp.float32)

        put(slot).start()
        return carry

    lax.fori_loop(begin, end, one, 0)
    for slot in range(max(begin, end - stages), end):
        put(slot).wait()


def legendre_sum(limits, data, bases, table, begin, end, before):
    slots, degrees, lats = table.shape
    levels = sum(d.shape[2] for d in data) // 2
    tiles = degrees // KTILE
    anywhere = pl.BlockSpec(memory_space=pl.ANY)
    vmem = pl.BlockSpec(memory_space=pltpu.VMEM)
    operands = [limits, *data, table] + ([] if before is None else [before])
    stages = min(4, end - begin)
    return pl.pallas_call(
        functools.partial(legendre_kernel, begin, end, tiles, bases, before is None),
        out_shape=jax.ShapeDtypeStruct((slots, 2, levels, degrees), jnp.float32),
        in_specs=[pl.BlockSpec(memory_space=pltpu.SMEM)]
        + [vmem] * len(data)
        + [anywhere] * (1 if before is None else 2),
        out_specs=anywhere,
        scratch_shapes=[
            pltpu.VMEM((6, degrees, lats), jnp.bfloat16),
            pltpu.VMEM((stages, 2, levels, degrees), jnp.float32),
            pltpu.SemaphoreType.DMA((6,)),
            pltpu.SemaphoreType.DMA((stages,)),
        ],
        input_output_aliases={} if before is None else {len(operands) - 1: 0},
        compiler_params=pltpu.CompilerParams(vmem_limit_bytes=VMEM),
        cost_estimate=pl.CostEstimate(
            flops=(end - begin) * degrees * lats * 4 * levels,
            bytes_accessed=(end - begin) * degrees * (lats + 8 * levels),
            transcendentals=0,
        ),
        name="legendre_sum",
    )(*operands)


def after(value, earlier):
    return value if earlier is None else lax.optimization_barrier((value, earlier))[0]


def spread(vorticity, chunk, lon_size, hop_order, earlier):
    hemis, lats, part = vorticity.shape[1:]
    me = lax.axis_index("lon")

    def piece(distance):
        level = chunk * lon_size + (me ^ distance)
        block = lax.dynamic_index_in_dim(vorticity, level, 0, keepdims=False) * PRESCALE
        return block.astype(jnp.float16).reshape(hemis * lats, part)

    got = {0: piece(0)}
    for distance in hop_order:
        sent = after(piece(distance), earlier and earlier[distance])
        got[distance] = lax.ppermute(sent, "lon", [(i, i ^ distance) for i in range(lon_size)])
    return got


def spread_whole(vorticity, chunk, lon_size, earlier):
    hemis, lats, part = vorticity.shape[1:]
    block = vorticity[chunk * lon_size : (chunk + 1) * lon_size] * PRESCALE
    block = after(block.astype(jnp.float16).reshape(lon_size, hemis * lats, part), earlier)
    return lax.all_to_all(block, "lon", split_axis=0, concat_axis=0, tiled=True)


def on_device(lat_size, lon_size, high, low, vorticity, legendre, wave_order):
    levels, hemis, lats, part = vorticity.shape
    slot_count = legendre.shape[0]
    devices = lat_size * lon_size
    waves = wave_order.astype(jnp.int32)
    lower, upper = waves % FIRST, waves // FIRST
    near = lower < HALF
    index = jnp.where(near, lower, FIRST - lower) * ROWS_K + jnp.where(near, 0, 2 * KEEP) + 2 * upper
    first_slot = lax.axis_index(("lat", "lon")) * slot_count
    limits = waves.shape[0] - lax.dynamic_slice_in_dim(waves, first_slot, slot_count)
    me = lax.axis_index("lon").reshape(1)
    chunks = levels // lon_size
    hop_order = sorted(range(1, lon_size), key=lambda d: (-(d >> 1), d & 1))

    got = spread(vorticity, 0, lon_size, hop_order, None)
    circles = [jnp.stack([got[i].astype(jnp.float32) for i in range(lon_size)])]
    for chunk in range(1, chunks):
        circles.append(spread_whole(vorticity, chunk, lon_size, tuple(got[d] for d in hop_order)).astype(jnp.float32))
    done = None
    arranged = []
    for chunk in range(chunks):
        parts = 2 if chunk == chunks - 1 else 1
        order = index.reshape(devices, parts, slot_count // parts).transpose(1, 0, 2).reshape(-1)
        pieces = []
        origin = me if chunk == 0 else jnp.zeros_like(me)
        results = fourier_slots(after(circles[chunk], done), origin, order, high, low, parts)
        done = results[0]
        for chosen in results:
            chosen = chosen.reshape(devices, slot_count // parts * 2, hemis * lats)
            moved = lax.all_to_all(chosen, ("lat", "lon"), split_axis=0, concat_axis=0, tiled=True)
            pieces.append(arrange(moved, lat_size, lon_size, slot_count // parts))
        arranged.append(pieces)
    result = None
    half = slot_count // 2
    for part in range(2):
        begin = part * half
        data = [pieces[part] if len(pieces) == 2 else pieces[0] for pieces in arranged]
        bases = [begin if len(pieces) == 2 else 0 for pieces in arranged]
        result = legendre_sum(limits, data, bases, legendre, begin, begin + half, result)
    return result


def solution(mesh):
    lat_size, lon_size = mesh.shape["lat"], mesh.shape["lon"]

    def whole(vorticity, legendre, wave_order):
        high, low = second_tables(vorticity.shape[3])
        body = functools.partial(on_device, lat_size, lon_size, high, low)
        return jax.shard_map(
            body,
            mesh=mesh,
            in_specs=(P(None, None, "lat", "lon"), P(("lat", "lon"), None, None), P()),
            out_specs=P(("lat", "lon"), None, None, None),
            check_vma=False,
        )(vorticity, legendre, wave_order)

    return whole
```

```python
import functools
import math

import jax
import jax.numpy as jnp
import numpy as np
from jax import lax
from jax.experimental import pallas as pl
from jax.experimental.pallas import tpu as pltpu
from jax.sharding import PartitionSpec as P

MW = 2048
FIRST = 64
LANES = 128
KEEP = MW // FIRST
HALF = FIRST // 2 + 1
ROWS_K = 4 * KEEP
KTILE = 256
PRESCALE = 8192.0
VMEM = 56 * 1024 * 1024
GROUP = 32
BUFFERS = 32


def second_tables(circle):
    b = np.arange(LANES)[None, :]
    scale = 1.0 / math.sqrt(circle) / PRESCALE
    table = np.zeros((HALF, 2, KEEP, 2, 2 * LANES), np.float64)
    for k in range(HALF):
        for side in range(2):
            first = k if side == 0 else FIRST - k
            m = (first + FIRST * np.arange(KEEP))[:, None]
            angle = 2.0 * np.pi / circle * ((m * b) % circle)
            c, s = np.cos(angle), np.sin(angle)
            sign = 1.0 if side == 0 else -1.0
            table[k, side, :, 0, :LANES] = c
            table[k, side, :, 0, LANES:] = sign * s
            table[k, side, :, 1, :LANES] = -s
            table[k, side, :, 1, LANES:] = sign * c
    table = (table * scale).astype(np.float32).reshape(HALF, ROWS_K, 2 * LANES)
    high = table.astype(jnp.bfloat16)
    low = (table - high.astype(np.float32)).astype(jnp.bfloat16)
    return high, low


def add(a, b):
    return (a[0] + b[0], a[1] + b[1])


def sub(a, b):
    return (a[0] - b[0], a[1] - b[1])


def minus_i(a):
    return (a[1], -a[0])


def times(a, angle):
    c, s = math.cos(angle), math.sin(angle)
    return (a[0] * c + a[1] * s, a[1] * c - a[0] * s)


def real_dft8(x):
    r = math.sqrt(0.5)
    s04, d04 = x[0] + x[4], x[0] - x[4]
    s26, d26 = x[2] + x[6], x[2] - x[6]
    s15, d15 = x[1] + x[5], x[1] - x[5]
    s37, d37 = x[3] + x[7], x[3] - x[7]
    even, odd = s04 + s26, s15 + s37
    p, q = r * (d15 - d37), r * (d15 + d37)
    return [
        (even + odd, None),
        (d04 + p, -(d26 + q)),
        (s04 - s26, -(s15 - s37)),
        (d04 - p, d26 - q),
        (even - odd, None),
    ]


def complex_dft8(x):
    r = math.sqrt(0.5)

    def dft4(a, b, c, d):
        s, t, u, v = add(a, c), sub(a, c), add(b, d), minus_i(sub(b, d))
        return [add(s, u), add(t, v), sub(s, u), sub(t, v)]

    even = dft4(x[0], x[2], x[4], x[6])
    odd = dft4(x[1], x[3], x[5], x[7])
    o1 = ((odd[1][0] + odd[1][1]) * r, (odd[1][1] - odd[1][0]) * r)
    o2 = minus_i(odd[2])
    o3 = ((odd[3][1] - odd[3][0]) * r, -(odd[3][0] + odd[3][1]) * r)
    turned = [odd[0], o1, o2, o3]
    return [add(e, o) for e, o in zip(even, turned)] + [sub(e, o) for e, o in zip(even, turned)]


def fourier_kernel(
    rows, slots, index_ref, me_ref, x_ref, high_ref, low_ref, out_ref, stage, y_high, y_low, full, picked
):
    me = me_ref[0]
    per_source = x_ref.shape[2] // LANES
    group = 16

    def put(k, row, value):
        for part in range(2):
            at = (k, pl.ds(row, group), pl.ds(part * LANES, LANES))
            v = value[part]
            if v is None:
                v = jnp.zeros((group, LANES), jnp.float32)
            h = v.astype(jnp.bfloat16)
            y_high[at] = h
            y_low[at] = (v - h.astype(jnp.float32)).astype(jnp.bfloat16)

    def first_step(step, carry):
        row = pl.multiple_of(step * group, group)
        for t in range(8):
            x = []
            for s in range(8):
                source, piece = divmod(8 * s + t, per_source)
                x.append(x_ref[me ^ source, pl.ds(row, group), pl.ds(piece * LANES, LANES)])
            for k1, (real, imag) in enumerate(real_dft8(x)):
                stage[t, k1, 0] = real
                if imag is not None:
                    stage[t, k1, 1] = imag
        for k2, value in enumerate(real_dft8([stage[t, 0, 0] for t in range(8)])):
            put(8 * k2, row, value)
        for k1 in range(1, 5):
            turned = []
            for t in range(8):
                angle = 2.0 * math.pi * t * k1 / FIRST
                if k1 == 4:
                    real = stage[t, k1, 0]
                    turned.append((real * math.cos(angle), real * -math.sin(angle)))
                else:
                    turned.append(times((stage[t, k1, 0], stage[t, k1, 1]), angle))
            for k2, value in enumerate(complex_dft8(turned)):
                k = k1 + 8 * k2
                if k < HALF:
                    put(k, row, value)
                elif k1 != 4:
                    put(FIRST - k, row, (value[0], -value[1]))
        return carry

    lax.fori_loop(0, rows // group, first_step, 0)

    def dot(a, b):
        return lax.dot_general(a, b, (((1,), (1,)), ((), ())), preferred_element_type=jnp.float32)

    def second_step(k, carry):
        at = pl.ds(pl.multiple_of(k * ROWS_K, ROWS_K), ROWS_K)
        full[at, :] = dot(high_ref[k], y_high[k]) + (dot(high_ref[k], y_low[k]) + dot(low_ref[k], y_high[k]))
        return carry

    lax.fori_loop(0, HALF, second_step, 0)

    def pick(step, carry):
        first = step * 8
        for i in range(8):
            at = pl.multiple_of(index_ref[first + i], 2)
            to = pl.multiple_of(step * 16, 16) + 2 * i
            picked[pl.ds(to, 2), :] = full[pl.ds(at, 2), :]
        return carry

    lax.fori_loop(0, slots // 8, pick, 0)
    out_ref[...] = picked[...].astype(jnp.bfloat16)


def fourier_slots(x, me, index, high, low):
    sources, rows, part = x.shape
    slots = index.shape[0]
    smem, vmem = pl.BlockSpec(memory_space=pltpu.SMEM), pl.BlockSpec(memory_space=pltpu.VMEM)
    return pl.pallas_call(
        functools.partial(fourier_kernel, rows, slots),
        out_shape=jax.ShapeDtypeStruct((slots * 2, rows), jnp.bfloat16),
        in_specs=[smem, smem, vmem, vmem, vmem],
        out_specs=vmem,
        scratch_shapes=[
            pltpu.VMEM((8, 5, 2, 16, LANES), jnp.float32),
            pltpu.VMEM((HALF, rows, 2 * LANES), jnp.bfloat16),
            pltpu.VMEM((HALF, rows, 2 * LANES), jnp.bfloat16),
            pltpu.VMEM((HALF * ROWS_K, rows), jnp.float32),
            pltpu.VMEM((slots * 2, rows), jnp.float32),
        ],
        compiler_params=pltpu.CompilerParams(vmem_limit_bytes=VMEM),
        cost_estimate=pl.CostEstimate(
            flops=6 * HALF * ROWS_K * rows * 2 * LANES, bytes_accessed=12 * 1024 * 1024, transcendentals=0
        ),
        name="fourier_slots",
    )(index, me, x, high, low)


def arrange(moved, slots, lat_size, lon_size):
    lats = moved.shape[2] // 2
    moved = moved.reshape(lat_size, lon_size, slots, 2, 2, lats)
    moved = jnp.transpose(moved, (2, 4, 3, 1, 0, 5))
    return moved.reshape(slots, 4 * lon_size, lat_size * lats)


def arrange_here(lat_size, lon_size, moved_ref, data_ref, sorted_rows):
    slots = data_ref.shape[0]
    rows = slots * 2
    for lat in range(lat_size):
        for lon in range(lon_size):
            block = moved_ref[lat * lon_size + lon].astype(jnp.float32)
            sorted_rows[lat, pl.ds(lon, rows, stride=lon_size), :] = block
    shape = (slots, 2 * lon_size, LANES)
    lane = lax.broadcasted_iota(jnp.int32, (rows * lon_size, LANES), 1)
    lower = lane < LANES // 2
    for pair in range(lat_size // 2):
        one, two = sorted_rows[2 * pair], sorted_rows[2 * pair + 1]
        north = jnp.where(lower, one, pltpu.roll(two, LANES // 2, 1))
        south = jnp.where(lower, pltpu.roll(one, LANES // 2, 1), two)
        lanes = pl.ds(pair * LANES, LANES)
        data_ref[:, 0 : 2 * lon_size, lanes] = north.reshape(shape).astype(jnp.bfloat16)
        data_ref[:, 2 * lon_size : 4 * lon_size, lanes] = south.reshape(shape).astype(jnp.bfloat16)


def legendre_kernel(tiles, level, sizes, has_before, limit_ref, moved_ref, table_ref, *refs):
    out_ref, held, staged, slot_of, tile_of, last_of, in_sems, out_sems, *scratch = refs[1 if has_before else 0 :]
    data_ref = scratch[0]
    incoming = pltpu.make_async_copy(moved_ref, scratch[2] if sizes else data_ref, scratch[-1])
    incoming.start()
    buffers, stages = held.shape[0], staged.shape[0]
    levels = staged.shape[2]
    half = 2 * levels
    begin, end = 0, table_ref.shape[0]

    def tile_count(slot):
        return lax.div(limit_ref[slot] + (KTILE - 1), KTILE)

    def fetch(slot, count):
        place = lax.rem(slot, buffers)
        rows = pl.ds(0, count * KTILE)
        return pltpu.make_async_copy(table_ref.at[slot, rows, :], held.at[place, rows, :], in_sems.at[place])

    def put(slot):
        place = lax.rem(slot, stages)
        target = out_ref.at[slot, :, pl.ds(level, levels), :]
        return pltpu.make_async_copy(staged.at[place], target, out_sems.at[place])

    def by_count(slot, act):
        count = tile_count(slot)

        def choose(low, high):
            if low == high:
                act(fetch(slot, low))
                return
            middle = (low + high) // 2
            lax.cond(count <= middle, lambda: choose(low, middle), lambda: choose(middle + 1, high))

        choose(1, tiles)

    def start(slot, carry):
        by_count(slot, lambda copy: copy.start())
        return carry

    lax.fori_loop(begin, min(begin + buffers, end), start, 0)

    def list_slot(slot, total):
        def list_tile(tile, carry):
            slot_of[total + tile] = slot
            tile_of[total + tile] = tile
            return carry

        count = tile_count(slot)
        lax.fori_loop(0, count, list_tile, 0)
        last_of[slot - begin] = total + count
        return total + count

    total = lax.fori_loop(begin, end, list_slot, 0)
    final = tile_of[total - 1]
    for i in range(GROUP):
        slot_of[total + i] = end - 1
        tile_of[total + i] = final

    incoming.wait()
    if sizes:
        arrange_here(*sizes, scratch[2], data_ref, scratch[1])

    degree = lax.broadcasted_iota(jnp.int32, (half, KTILE), 1)
    parity = (1 - 2 * (degree % 2)).astype(jnp.float32)

    def enter(slot, carry):
        by_count(slot, lambda copy: copy.wait())

        @pl.when(slot - begin >= stages)
        def _():
            put(slot - stages).wait()

        def clear(tile, carry):
            cols = pl.ds(pl.multiple_of(tile * KTILE, KTILE), KTILE)
            staged[lax.rem(slot, stages), :, :, cols] = jnp.zeros((2, levels, KTILE), jnp.float32)
            return carry

        lax.fori_loop(tile_count(slot), tiles, clear, 0)
        return carry

    def leave(slot, carry):
        put(slot).start()
        return carry

    def one_tile(item):
        slot, tile = slot_of[item], tile_of[item]
        place, stage = lax.rem(slot, buffers), lax.rem(slot, stages)
        cols = pl.ds(pl.multiple_of(tile * KTILE, KTILE), KTILE)
        product = lax.dot_general(
            data_ref[slot],
            held[place, cols, :],
            (((1,), (1,)), ((), ())),
            preferred_element_type=jnp.float32,
        )
        both = product[:half] + parity * product[half:]
        both = jnp.where(degree < limit_ref[slot] - tile * KTILE, both, 0.0)
        for c in range(2):
            staged[stage, c, :, cols] = both[c * levels : (c + 1) * levels]

    def one_group(group, carry):
        fetched, entered, left = carry
        item = group * GROUP
        newest = slot_of[item + GROUP - 1]
        wanted = jnp.minimum(slot_of[item] + buffers, end)
        lax.fori_loop(fetched, wanted, start, 0)
        lax.fori_loop(entered, newest + 1, enter, 0)
        for i in range(GROUP):
            one_tile(item + i)
        done = jnp.where(last_of[newest - begin] <= item + GROUP, newest + 1, newest)
        lax.fori_loop(left, done, leave, 0)
        return jnp.maximum(fetched, wanted), newest + 1, done

    groups = lax.div(total + GROUP - 1, GROUP)
    lax.fori_loop(0, groups, one_group, (min(begin + buffers, end), begin, begin))
    for slot in range(max(begin, end - stages), end):
        put(slot).wait()


def legendre_sum(limits, moved, table, level, levels, total_levels, lat_size, lon_size, before):
    slots, degrees, lats = table.shape
    tiles = degrees // KTILE
    anywhere = pl.BlockSpec(memory_space=pl.ANY)
    here = moved.shape[2] == LANES and levels == 8
    if not here:
        moved = arrange(moved, slots, lat_size, lon_size)
    operands = [limits, moved, table] + ([] if before is None else [before])
    items = slots * tiles + GROUP
    data = [pltpu.VMEM((slots, 4 * levels, lats), jnp.bfloat16)]
    if here:
        data.append(pltpu.VMEM((lat_size, slots * 2 * levels, LANES), jnp.float32))
        data.append(pltpu.VMEM(moved.shape, jnp.bfloat16))
    return pl.pallas_call(
        functools.partial(
            legendre_kernel, tiles, level, (lat_size, lon_size) if here else None, before is not None
        ),
        out_shape=jax.ShapeDtypeStruct((slots, 2, total_levels, degrees), jnp.float32),
        in_specs=[pl.BlockSpec(memory_space=pltpu.SMEM)] + [anywhere] * (2 if before is None else 3),
        out_specs=anywhere,
        scratch_shapes=[
            pltpu.VMEM((BUFFERS, degrees, lats), jnp.bfloat16),
            pltpu.VMEM((GROUP, 2, levels, degrees), jnp.float32),
            pltpu.SMEM((items,), jnp.int32),
            pltpu.SMEM((items,), jnp.int32),
            pltpu.SMEM((slots,), jnp.int32),
            pltpu.SemaphoreType.DMA((BUFFERS,)),
            pltpu.SemaphoreType.DMA((GROUP,)),
        ]
        + data
        + [pltpu.SemaphoreType.DMA],
        input_output_aliases={} if before is None else {3: 0},
        compiler_params=pltpu.CompilerParams(vmem_limit_bytes=VMEM),
        cost_estimate=pl.CostEstimate(
            flops=slots * degrees * lats * 4 * levels,
            bytes_accessed=slots * degrees * (lats + 8 * levels),
            transcendentals=0,
        ),
        name="legendre_sum",
    )(*operands)


def after(value, earlier):
    return value if earlier is None else lax.optimization_barrier((value, earlier))[0]


def spread(vorticity, chunk, lon_size, hop_order):
    hemis, lats, part = vorticity.shape[1:]
    me = lax.axis_index("lon")

    def piece(distance, source):
        level = chunk * lon_size + (me ^ distance)
        block = lax.dynamic_index_in_dim(source, level, 0, keepdims=False) * PRESCALE
        return block.astype(jnp.float16).reshape(hemis * lats, part)

    got, source, rounded = {}, vorticity, None
    for turn, distance in enumerate(hop_order):
        if turn in (1, 3):
            source = after(source, rounded)
        rounded = piece(distance, source)
        got[distance] = lax.ppermute(rounded, "lon", [(i, i ^ distance) for i in range(lon_size)])
    got[0] = piece(0, source)
    return got


def spread_whole(vorticity, chunk, lon_size, earlier):
    hemis, lats, part = vorticity.shape[1:]
    block = vorticity[chunk * lon_size : (chunk + 1) * lon_size] * PRESCALE
    block = after(block.astype(jnp.float16).reshape(lon_size, hemis * lats, part), earlier)
    return lax.all_to_all(block, "lon", split_axis=0, concat_axis=0, tiled=True)


def on_device(lat_size, lon_size, high, low, vorticity, legendre, wave_order):
    levels, hemis, lats, part = vorticity.shape
    slot_count = legendre.shape[0]
    devices = lat_size * lon_size
    waves = wave_order.astype(jnp.int32)
    lower, upper = waves % FIRST, waves // FIRST
    near = lower < HALF
    index = jnp.where(near, lower, FIRST - lower) * ROWS_K + jnp.where(near, 0, 2 * KEEP) + 2 * upper
    first_slot = lax.axis_index(("lat", "lon")) * slot_count
    limits = waves.shape[0] - lax.dynamic_slice_in_dim(waves, first_slot, slot_count)
    me = lax.axis_index("lon").reshape(1)
    chunks = levels // lon_size
    hop_order = sorted(range(1, lon_size), key=lambda d: (-(d >> 1), d & 1))

    got = spread(vorticity, 0, lon_size, hop_order)
    circles = [jnp.stack([got[i].astype(jnp.float32) for i in range(lon_size)])]
    for chunk in range(1, chunks):
        circles.append(spread_whole(vorticity, chunk, lon_size, tuple(got[d] for d in hop_order)).astype(jnp.float32))
    done = None
    moved = []
    for chunk in range(chunks):
        origin = me if chunk == 0 else jnp.zeros_like(me)
        chosen = fourier_slots(after(circles[chunk], done), origin, index, high, low)
        done = chosen
        chosen = chosen.reshape(devices, slot_count * 2, hemis * lats)
        moved.append(lax.all_to_all(chosen, ("lat", "lon"), split_axis=0, concat_axis=0, tiled=True))
    result = None
    for chunk in range(chunks):
        first = chunk * lon_size
        result = legendre_sum(limits, moved[chunk], legendre, first, lon_size, levels, lat_size, lon_size, result)
    return result


def solution(mesh):
    lat_size, lon_size = mesh.shape["lat"], mesh.shape["lon"]

    def whole(vorticity, legendre, wave_order):
        high, low = second_tables(vorticity.shape[3])
        body = functools.partial(on_device, lat_size, lon_size, high, low)
        return jax.shard_map(
            body,
            mesh=mesh,
            in_specs=(P(None, None, "lat", "lon"), P(("lat", "lon"), None, None), P()),
            out_specs=P(("lat", "lon"), None, None, None),
            check_vma=False,
        )(vorticity, legendre, wave_order)

    return whole
```

```python
import functools
import math

import jax
import jax.numpy as jnp
import numpy as np
from jax import lax
from jax.experimental import pallas as pl
from jax.experimental.pallas import tpu as pltpu
from jax.sharding import PartitionSpec as P

MW = 2048
FIRST = 64
LANES = 128
KEEP = MW // FIRST
HALF = FIRST // 2 + 1
ROWS_K = 4 * KEEP
KTILE = 256
PRESCALE = 8192.0
VMEM = 56 * 1024 * 1024
GROUP = 32
BUFFERS = 32


def second_tables(circle):
    b = np.arange(LANES)[None, :]
    scale = 1.0 / math.sqrt(circle) / PRESCALE
    table = np.zeros((HALF, 2, KEEP, 2, 2 * LANES), np.float64)
    for k in range(HALF):
        for side in range(2):
            first = k if side == 0 else FIRST - k
            m = (first + FIRST * np.arange(KEEP))[:, None]
            angle = 2.0 * np.pi / circle * ((m * b) % circle)
            c, s = np.cos(angle), np.sin(angle)
            sign = 1.0 if side == 0 else -1.0
            table[k, side, :, 0, :LANES] = c
            table[k, side, :, 0, LANES:] = sign * s
            table[k, side, :, 1, :LANES] = -s
            table[k, side, :, 1, LANES:] = sign * c
    table = (table * scale).astype(np.float32).reshape(HALF, ROWS_K, 2 * LANES)
    high = table.astype(jnp.bfloat16)
    low = (table - high.astype(np.float32)).astype(jnp.bfloat16)
    return high, low


def add(a, b):
    return (a[0] + b[0], a[1] + b[1])


def sub(a, b):
    return (a[0] - b[0], a[1] - b[1])


def minus_i(a):
    return (a[1], -a[0])


def times(a, angle):
    c, s = math.cos(angle), math.sin(angle)
    return (a[0] * c + a[1] * s, a[1] * c - a[0] * s)


def real_dft8(x):
    r = math.sqrt(0.5)
    s04, d04 = x[0] + x[4], x[0] - x[4]
    s26, d26 = x[2] + x[6], x[2] - x[6]
    s15, d15 = x[1] + x[5], x[1] - x[5]
    s37, d37 = x[3] + x[7], x[3] - x[7]
    even, odd = s04 + s26, s15 + s37
    p, q = r * (d15 - d37), r * (d15 + d37)
    return [
        (even + odd, None),
        (d04 + p, -(d26 + q)),
        (s04 - s26, -(s15 - s37)),
        (d04 - p, d26 - q),
        (even - odd, None),
    ]


def complex_dft8(x):
    r = math.sqrt(0.5)

    def dft4(a, b, c, d):
        s, t, u, v = add(a, c), sub(a, c), add(b, d), minus_i(sub(b, d))
        return [add(s, u), add(t, v), sub(s, u), sub(t, v)]

    even = dft4(x[0], x[2], x[4], x[6])
    odd = dft4(x[1], x[3], x[5], x[7])
    o1 = ((odd[1][0] + odd[1][1]) * r, (odd[1][1] - odd[1][0]) * r)
    o2 = minus_i(odd[2])
    o3 = ((odd[3][1] - odd[3][0]) * r, -(odd[3][0] + odd[3][1]) * r)
    turned = [odd[0], o1, o2, o3]
    return [add(e, o) for e, o in zip(even, turned)] + [sub(e, o) for e, o in zip(even, turned)]


def fourier_kernel(
    rows, slots, index_ref, me_ref, x_ref, high_ref, low_ref, out_ref, stage, y_high, y_low, full, picked
):
    me = me_ref[0]
    per_source = x_ref.shape[2] // LANES
    group = 16

    def put(k, row, value):
        for part in range(2):
            at = (k, pl.ds(row, group), pl.ds(part * LANES, LANES))
            v = value[part]
            if v is None:
                v = jnp.zeros((group, LANES), jnp.float32)
            h = v.astype(jnp.bfloat16)
            y_high[at] = h
            y_low[at] = (v - h.astype(jnp.float32)).astype(jnp.bfloat16)

    def first_step(step, carry):
        row = pl.multiple_of(step * group, group)
        for t in range(8):
            x = []
            for s in range(8):
                source, piece = divmod(8 * s + t, per_source)
                x.append(x_ref[me ^ source, pl.ds(row, group), pl.ds(piece * LANES, LANES)])
            for k1, (real, imag) in enumerate(real_dft8(x)):
                stage[t, k1, 0] = real
                if imag is not None:
                    stage[t, k1, 1] = imag
        for k2, value in enumerate(real_dft8([stage[t, 0, 0] for t in range(8)])):
            put(8 * k2, row, value)
        for k1 in range(1, 5):
            turned = []
            for t in range(8):
                angle = 2.0 * math.pi * t * k1 / FIRST
                if k1 == 4:
                    real = stage[t, k1, 0]
                    turned.append((real * math.cos(angle), real * -math.sin(angle)))
                else:
                    turned.append(times((stage[t, k1, 0], stage[t, k1, 1]), angle))
            for k2, value in enumerate(complex_dft8(turned)):
                k = k1 + 8 * k2
                if k < HALF:
                    put(k, row, value)
                elif k1 != 4:
                    put(FIRST - k, row, (value[0], -value[1]))
        return carry

    lax.fori_loop(0, rows // group, first_step, 0)

    def dot(a, b):
        return lax.dot_general(a, b, (((1,), (1,)), ((), ())), preferred_element_type=jnp.float32)

    def second_step(k, carry):
        at = pl.ds(pl.multiple_of(k * ROWS_K, ROWS_K), ROWS_K)
        full[at, :] = dot(high_ref[k], y_high[k]) + (dot(high_ref[k], y_low[k]) + dot(low_ref[k], y_high[k]))
        return carry

    lax.fori_loop(0, HALF, second_step, 0)

    def pick(step, carry):
        first = step * 8
        for i in range(8):
            at = pl.multiple_of(index_ref[first + i], 2)
            to = pl.multiple_of(step * 16, 16) + 2 * i
            picked[pl.ds(to, 2), :] = full[pl.ds(at, 2), :]
        return carry

    lax.fori_loop(0, slots // 8, pick, 0)
    out_ref[...] = picked[...].astype(jnp.bfloat16)


def fourier_slots(x, me, index, high, low):
    sources, rows, part = x.shape
    slots = index.shape[0]
    smem, vmem = pl.BlockSpec(memory_space=pltpu.SMEM), pl.BlockSpec(memory_space=pltpu.VMEM)
    return pl.pallas_call(
        functools.partial(fourier_kernel, rows, slots),
        out_shape=jax.ShapeDtypeStruct((slots * 2, rows), jnp.bfloat16),
        in_specs=[smem, smem, vmem, vmem, vmem],
        out_specs=vmem,
        scratch_shapes=[
            pltpu.VMEM((8, 5, 2, 16, LANES), jnp.float32),
            pltpu.VMEM((HALF, rows, 2 * LANES), jnp.bfloat16),
            pltpu.VMEM((HALF, rows, 2 * LANES), jnp.bfloat16),
            pltpu.VMEM((HALF * ROWS_K, rows), jnp.float32),
            pltpu.VMEM((slots * 2, rows), jnp.float32),
        ],
        compiler_params=pltpu.CompilerParams(vmem_limit_bytes=VMEM),
        cost_estimate=pl.CostEstimate(
            flops=6 * HALF * ROWS_K * rows * 2 * LANES, bytes_accessed=12 * 1024 * 1024, transcendentals=0
        ),
        name="fourier_slots",
    )(index, me, x, high, low)


def arrange(moved, slots, lat_size, lon_size):
    lats = moved.shape[2] // 2
    moved = moved.reshape(lat_size, lon_size, slots, 2, 2, lats)
    moved = jnp.transpose(moved, (2, 4, 3, 1, 0, 5))
    return moved.reshape(slots, 4 * lon_size, lat_size * lats)


def arrange_here(lat_size, lon_size, moved_ref, data_ref, sorted_rows):
    slots = data_ref.shape[0]
    rows = slots * 2
    for lat in range(lat_size):
        for lon in range(lon_size):
            block = moved_ref[lat * lon_size + lon].astype(jnp.float32)
            sorted_rows[lat, pl.ds(lon, rows, stride=lon_size), :] = block
    shape = (slots, 2 * lon_size, LANES)
    lane = lax.broadcasted_iota(jnp.int32, (rows * lon_size, LANES), 1)
    lower = lane < LANES // 2
    for pair in range(lat_size // 2):
        one, two = sorted_rows[2 * pair], sorted_rows[2 * pair + 1]
        north = jnp.where(lower, one, pltpu.roll(two, LANES // 2, 1))
        south = jnp.where(lower, pltpu.roll(one, LANES // 2, 1), two)
        lanes = pl.ds(pair * LANES, LANES)
        data_ref[:, 0 : 2 * lon_size, lanes] = north.reshape(shape).astype(jnp.bfloat16)
        data_ref[:, 2 * lon_size : 4 * lon_size, lanes] = south.reshape(shape).astype(jnp.bfloat16)


def legendre_kernel(tiles, level, sizes, has_before, limit_ref, moved_ref, table_ref, *refs):
    out_ref, held, staged, slot_of, tile_of, last_of, in_sems, out_sems, *scratch = refs[1 if has_before else 0 :]
    data_ref = scratch[0]
    incoming = pltpu.make_async_copy(moved_ref, scratch[2] if sizes else data_ref, scratch[-1])
    incoming.start()
    buffers, stages = held.shape[0], staged.shape[0]
    levels = staged.shape[2]
    half = 2 * levels
    begin, end = 0, table_ref.shape[0]

    def tile_count(slot):
        return lax.div(limit_ref[slot] + (KTILE - 1), KTILE)

    def fetch(slot, count):
        place = lax.rem(slot, buffers)
        rows = pl.ds(0, count * KTILE)
        return pltpu.make_async_copy(table_ref.at[slot, rows, :], held.at[place, rows, :], in_sems.at[place])

    def put(slot):
        place = lax.rem(slot, stages)
        target = out_ref.at[slot, :, pl.ds(level, levels), :]
        return pltpu.make_async_copy(staged.at[place], target, out_sems.at[place])

    def by_count(slot, act):
        count = tile_count(slot)

        def choose(low, high):
            if low == high:
                act(fetch(slot, low))
                return
            middle = (low + high) // 2
            lax.cond(count <= middle, lambda: choose(low, middle), lambda: choose(middle + 1, high))

        choose(1, tiles)

    def start(slot, carry):
        by_count(slot, lambda copy: copy.start())
        return carry

    lax.fori_loop(begin, min(begin + buffers, end), start, 0)

    def list_slot(slot, total):
        def list_tile(tile, carry):
            slot_of[total + tile] = slot
            tile_of[total + tile] = tile
            return carry

        count = tile_count(slot)
        lax.fori_loop(0, count, list_tile, 0)
        last_of[slot - begin] = total + count
        return total + count

    total = lax.fori_loop(begin, end, list_slot, 0)
    final = tile_of[total - 1]
    for i in range(GROUP):
        slot_of[total + i] = end - 1
        tile_of[total + i] = final

    incoming.wait()
    if sizes:
        arrange_here(*sizes, scratch[2], data_ref, scratch[1])

    degree = lax.broadcasted_iota(jnp.int32, (half, KTILE), 1)
    parity = (1 - 2 * (degree % 2)).astype(jnp.float32)

    def enter(slot, carry):
        by_count(slot, lambda copy: copy.wait())

        @pl.when(slot - begin >= stages)
        def _():
            put(slot - stages).wait()

        def clear(tile, carry):
            cols = pl.ds(pl.multiple_of(tile * KTILE, KTILE), KTILE)
            staged[lax.rem(slot, stages), :, :, cols] = jnp.zeros((2, levels, KTILE), jnp.float32)
            return carry

        lax.fori_loop(tile_count(slot), tiles, clear, 0)
        return carry

    def leave(slot, carry):
        put(slot).start()
        return carry

    def one_tile(item):
        slot, tile = slot_of[item], tile_of[item]
        place, stage = lax.rem(slot, buffers), lax.rem(slot, stages)
        cols = pl.ds(pl.multiple_of(tile * KTILE, KTILE), KTILE)
        product = lax.dot_general(
            data_ref[slot],
            held[place, cols, :],
            (((1,), (1,)), ((), ())),
            preferred_element_type=jnp.float32,
        )
        both = product[:half] + parity * product[half:]
        both = jnp.where(degree < limit_ref[slot] - tile * KTILE, both, 0.0)
        for c in range(2):
            staged[stage, c, :, cols] = both[c * levels : (c + 1) * levels]

    def one_group(group, carry):
        fetched, entered, left = carry
        item = group * GROUP
        newest = slot_of[item + GROUP - 1]
        wanted = jnp.minimum(slot_of[item] + buffers, end)
        lax.fori_loop(fetched, wanted, start, 0)
        lax.fori_loop(entered, newest + 1, enter, 0)
        for i in range(GROUP):
            one_tile(item + i)
        done = jnp.where(last_of[newest - begin] <= item + GROUP, newest + 1, newest)
        lax.fori_loop(left, done, leave, 0)
        return jnp.maximum(fetched, wanted), newest + 1, done

    groups = lax.div(total + GROUP - 1, GROUP)
    lax.fori_loop(0, groups, one_group, (min(begin + buffers, end), begin, begin))
    for slot in range(max(begin, end - stages), end):
        put(slot).wait()


def legendre_sum(limits, moved, table, level, levels, total_levels, lat_size, lon_size, before):
    slots, degrees, lats = table.shape
    tiles = degrees // KTILE
    anywhere = pl.BlockSpec(memory_space=pl.ANY)
    here = moved.shape[2] == LANES and levels == 8
    if not here:
        moved = arrange(moved, slots, lat_size, lon_size)
    operands = [limits, moved, table] + ([] if before is None else [before])
    items = slots * tiles + GROUP
    data = [pltpu.VMEM((slots, 4 * levels, lats), jnp.bfloat16)]
    if here:
        data.append(pltpu.VMEM((lat_size, slots * 2 * levels, LANES), jnp.float32))
        data.append(pltpu.VMEM(moved.shape, jnp.bfloat16))
    return pl.pallas_call(
        functools.partial(
            legendre_kernel, tiles, level, (lat_size, lon_size) if here else None, before is not None
        ),
        out_shape=jax.ShapeDtypeStruct((slots, 2, total_levels, degrees), jnp.float32),
        in_specs=[pl.BlockSpec(memory_space=pltpu.SMEM)] + [anywhere] * (2 if before is None else 3),
        out_specs=anywhere,
        scratch_shapes=[
            pltpu.VMEM((BUFFERS, degrees, lats), jnp.bfloat16),
            pltpu.VMEM((GROUP, 2, levels, degrees), jnp.float32),
            pltpu.SMEM((items,), jnp.int32),
            pltpu.SMEM((items,), jnp.int32),
            pltpu.SMEM((slots,), jnp.int32),
            pltpu.SemaphoreType.DMA((BUFFERS,)),
            pltpu.SemaphoreType.DMA((GROUP,)),
        ]
        + data
        + [pltpu.SemaphoreType.DMA],
        input_output_aliases={} if before is None else {3: 0},
        compiler_params=pltpu.CompilerParams(vmem_limit_bytes=VMEM),
        cost_estimate=pl.CostEstimate(
            flops=slots * degrees * lats * 4 * levels,
            bytes_accessed=slots * degrees * (lats + 8 * levels),
            transcendentals=0,
        ),
        name="legendre_sum",
    )(*operands)


def after(value, earlier):
    return value if earlier is None else lax.optimization_barrier((value, earlier))[0]


def spread(vorticity, chunk, lon_size, hop_order):
    hemis, lats, part = vorticity.shape[1:]
    me = lax.axis_index("lon")

    def piece(distance, source):
        level = chunk * lon_size + (me ^ distance)
        block = lax.dynamic_index_in_dim(source, level, 0, keepdims=False) * PRESCALE
        return block.astype(jnp.float16).reshape(hemis * lats, part)

    got, source, rounded = {}, vorticity, None
    for turn, distance in enumerate(hop_order):
        if turn in (1, 3):
            source = after(source, rounded)
        rounded = piece(distance, source)
        got[distance] = lax.ppermute(rounded, "lon", [(i, i ^ distance) for i in range(lon_size)])
    got[0] = piece(0, source)
    return got


def spread_whole(vorticity, chunk, lon_size, earlier):
    hemis, lats, part = vorticity.shape[1:]
    block = vorticity[chunk * lon_size : (chunk + 1) * lon_size] * PRESCALE
    block = after(block.astype(jnp.float16).reshape(lon_size, hemis * lats, part), earlier)
    return lax.all_to_all(block, "lon", split_axis=0, concat_axis=0, tiled=True)


def on_device(lat_size, lon_size, high, low, vorticity, legendre, wave_order):
    levels, hemis, lats, part = vorticity.shape
    slot_count = legendre.shape[0]
    devices = lat_size * lon_size
    waves = wave_order.astype(jnp.int32)
    lower, upper = waves % FIRST, waves // FIRST
    near = lower < HALF
    index = jnp.where(near, lower, FIRST - lower) * ROWS_K + jnp.where(near, 0, 2 * KEEP) + 2 * upper
    first_slot = lax.axis_index(("lat", "lon")) * slot_count
    limits = waves.shape[0] - lax.dynamic_slice_in_dim(waves, first_slot, slot_count)
    me = lax.axis_index("lon").reshape(1)
    chunks = levels // lon_size
    hop_order = sorted(range(1, lon_size), key=lambda d: (d & 1, -(d >> 1)))

    got = spread(vorticity, 0, lon_size, hop_order)
    circles = [jnp.stack([got[i].astype(jnp.float32) for i in range(lon_size)])]
    for chunk in range(1, chunks):
        circles.append(spread_whole(vorticity, chunk, lon_size, tuple(got[d] for d in hop_order)).astype(jnp.float32))
    done = None
    moved = []
    for chunk in range(chunks):
        origin = me if chunk == 0 else jnp.zeros_like(me)
        chosen = fourier_slots(after(circles[chunk], done), origin, index, high, low)
        done = chosen
        chosen = chosen.reshape(devices, slot_count * 2, hemis * lats)
        moved.append(lax.all_to_all(chosen, ("lat", "lon"), split_axis=0, concat_axis=0, tiled=True))
    result = None
    for chunk in range(chunks):
        first = chunk * lon_size
        result = legendre_sum(limits, moved[chunk], legendre, first, lon_size, levels, lat_size, lon_size, result)
    return result


def solution(mesh):
    lat_size, lon_size = mesh.shape["lat"], mesh.shape["lon"]

    def whole(vorticity, legendre, wave_order):
        high, low = second_tables(vorticity.shape[3])
        body = functools.partial(on_device, lat_size, lon_size, high, low)
        return jax.shard_map(
            body,
            mesh=mesh,
            in_specs=(P(None, None, "lat", "lon"), P(("lat", "lon"), None, None), P()),
            out_specs=P(("lat", "lon"), None, None, None),
            check_vma=False,
        )(vorticity, legendre, wave_order)

    return whole
```

```python
import functools
import math

import jax
import jax.numpy as jnp
import numpy as np
from jax import lax
from jax.experimental import pallas as pl
from jax.experimental.pallas import tpu as pltpu
from jax.sharding import PartitionSpec as P

MW = 2048
FIRST = 64
LANES = 128
KEEP = MW // FIRST
HALF = FIRST // 2 + 1
ROWS_K = 4 * KEEP
KTILE = 256
PRESCALE = 8192.0
VMEM = 56 * 1024 * 1024
GROUP = 32
BUFFERS = 32


def second_tables(circle):
    b = np.arange(LANES)[None, :]
    scale = 1.0 / math.sqrt(circle) / PRESCALE
    table = np.zeros((HALF, 2, KEEP, 2, 2 * LANES), np.float64)
    for k in range(HALF):
        for side in range(2):
            first = k if side == 0 else FIRST - k
            m = (first + FIRST * np.arange(KEEP))[:, None]
            angle = 2.0 * np.pi / circle * ((m * b) % circle)
            c, s = np.cos(angle), np.sin(angle)
            sign = 1.0 if side == 0 else -1.0
            table[k, side, :, 0, :LANES] = c
            table[k, side, :, 0, LANES:] = sign * s
            table[k, side, :, 1, :LANES] = -s
            table[k, side, :, 1, LANES:] = sign * c
    table = (table * scale).astype(np.float32).reshape(HALF, ROWS_K, 2 * LANES)
    high = table.astype(jnp.bfloat16)
    low = (table - high.astype(np.float32)).astype(jnp.bfloat16)
    return high, low


def add(a, b):
    return (a[0] + b[0], a[1] + b[1])


def sub(a, b):
    return (a[0] - b[0], a[1] - b[1])


def minus_i(a):
    return (a[1], -a[0])


def times(a, angle):
    c, s = math.cos(angle), math.sin(angle)
    return (a[0] * c + a[1] * s, a[1] * c - a[0] * s)


def real_dft8(x):
    r = math.sqrt(0.5)
    s04, d04 = x[0] + x[4], x[0] - x[4]
    s26, d26 = x[2] + x[6], x[2] - x[6]
    s15, d15 = x[1] + x[5], x[1] - x[5]
    s37, d37 = x[3] + x[7], x[3] - x[7]
    even, odd = s04 + s26, s15 + s37
    p, q = r * (d15 - d37), r * (d15 + d37)
    return [
        (even + odd, None),
        (d04 + p, -(d26 + q)),
        (s04 - s26, -(s15 - s37)),
        (d04 - p, d26 - q),
        (even - odd, None),
    ]


def complex_dft8(x):
    r = math.sqrt(0.5)

    def dft4(a, b, c, d):
        s, t, u, v = add(a, c), sub(a, c), add(b, d), minus_i(sub(b, d))
        return [add(s, u), add(t, v), sub(s, u), sub(t, v)]

    even = dft4(x[0], x[2], x[4], x[6])
    odd = dft4(x[1], x[3], x[5], x[7])
    o1 = ((odd[1][0] + odd[1][1]) * r, (odd[1][1] - odd[1][0]) * r)
    o2 = minus_i(odd[2])
    o3 = ((odd[3][1] - odd[3][0]) * r, -(odd[3][0] + odd[3][1]) * r)
    turned = [odd[0], o1, o2, o3]
    return [add(e, o) for e, o in zip(even, turned)] + [sub(e, o) for e, o in zip(even, turned)]


def fourier_kernel(
    rows, slots, index_ref, me_ref, x_ref, high_ref, low_ref, out_ref, stage, y_high, y_low, full, picked
):
    me = me_ref[0]
    per_source = x_ref.shape[2] // LANES
    group = 16

    def put(k, row, value):
        for part in range(2):
            at = (k, pl.ds(row, group), pl.ds(part * LANES, LANES))
            v = value[part]
            if v is None:
                v = jnp.zeros((group, LANES), jnp.float32)
            h = v.astype(jnp.bfloat16)
            y_high[at] = h
            y_low[at] = (v - h.astype(jnp.float32)).astype(jnp.bfloat16)

    def first_step(step, carry):
        row = pl.multiple_of(step * group, group)
        for t in range(8):
            x = []
            for s in range(8):
                source, piece = divmod(8 * s + t, per_source)
                x.append(x_ref[me ^ source, pl.ds(row, group), pl.ds(piece * LANES, LANES)])
            for k1, (real, imag) in enumerate(real_dft8(x)):
                stage[t, k1, 0] = real
                if imag is not None:
                    stage[t, k1, 1] = imag
        for k2, value in enumerate(real_dft8([stage[t, 0, 0] for t in range(8)])):
            put(8 * k2, row, value)
        for k1 in range(1, 5):
            turned = []
            for t in range(8):
                angle = 2.0 * math.pi * t * k1 / FIRST
                if k1 == 4:
                    real = stage[t, k1, 0]
                    turned.append((real * math.cos(angle), real * -math.sin(angle)))
                else:
                    turned.append(times((stage[t, k1, 0], stage[t, k1, 1]), angle))
            for k2, value in enumerate(complex_dft8(turned)):
                k = k1 + 8 * k2
                if k < HALF:
                    put(k, row, value)
                elif k1 != 4:
                    put(FIRST - k, row, (value[0], -value[1]))
        return carry

    lax.fori_loop(0, rows // group, first_step, 0)

    def dot(a, b):
        return lax.dot_general(a, b, (((1,), (1,)), ((), ())), preferred_element_type=jnp.float32)

    def second_step(k, carry):
        at = pl.ds(pl.multiple_of(k * ROWS_K, ROWS_K), ROWS_K)
        full[at, :] = dot(high_ref[k], y_high[k]) + (dot(high_ref[k], y_low[k]) + dot(low_ref[k], y_high[k]))
        return carry

    lax.fori_loop(0, HALF, second_step, 0)

    def pick(step, carry):
        first = step * 8
        for i in range(8):
            at = pl.multiple_of(index_ref[first + i], 2)
            to = pl.multiple_of(step * 16, 16) + 2 * i
            picked[pl.ds(to, 2), :] = full[pl.ds(at, 2), :]
        return carry

    lax.fori_loop(0, slots // 8, pick, 0)
    out_ref[...] = picked[...].astype(jnp.bfloat16)


def fourier_slots(x, me, index, high, low):
    sources, rows, part = x.shape
    slots = index.shape[0]
    smem, vmem = pl.BlockSpec(memory_space=pltpu.SMEM), pl.BlockSpec(memory_space=pltpu.VMEM)
    return pl.pallas_call(
        functools.partial(fourier_kernel, rows, slots),
        out_shape=jax.ShapeDtypeStruct((slots * 2, rows), jnp.bfloat16),
        in_specs=[smem, smem, vmem, vmem, vmem],
        out_specs=vmem,
        scratch_shapes=[
            pltpu.VMEM((8, 5, 2, 16, LANES), jnp.float32),
            pltpu.VMEM((HALF, rows, 2 * LANES), jnp.bfloat16),
            pltpu.VMEM((HALF, rows, 2 * LANES), jnp.bfloat16),
            pltpu.VMEM((HALF * ROWS_K, rows), jnp.float32),
            pltpu.VMEM((slots * 2, rows), jnp.float32),
        ],
        compiler_params=pltpu.CompilerParams(vmem_limit_bytes=VMEM),
        cost_estimate=pl.CostEstimate(
            flops=6 * HALF * ROWS_K * rows * 2 * LANES, bytes_accessed=12 * 1024 * 1024, transcendentals=0
        ),
        name="fourier_slots",
    )(index, me, x, high, low)


def arrange(moved, slots, lat_size, lon_size):
    lats = moved.shape[2] // 2
    moved = moved.reshape(lat_size, lon_size, slots, 2, 2, lats)
    moved = jnp.transpose(moved, (2, 4, 3, 1, 0, 5))
    return moved.reshape(slots, 4 * lon_size, lat_size * lats)


def arrange_here(lat_size, lon_size, moved_ref, data_ref, sorted_rows):
    slots = data_ref.shape[0]
    rows = slots * 2
    for lat in range(lat_size):
        for lon in range(lon_size):
            block = moved_ref[lat * lon_size + lon].astype(jnp.float32)
            sorted_rows[lat, pl.ds(lon, rows, stride=lon_size), :] = block
    shape = (slots, 2 * lon_size, LANES)
    lane = lax.broadcasted_iota(jnp.int32, (rows * lon_size, LANES), 1)
    lower = lane < LANES // 2
    for pair in range(lat_size // 2):
        one, two = sorted_rows[2 * pair], sorted_rows[2 * pair + 1]
        north = jnp.where(lower, one, pltpu.roll(two, LANES // 2, 1))
        south = jnp.where(lower, pltpu.roll(one, LANES // 2, 1), two)
        lanes = pl.ds(pair * LANES, LANES)
        data_ref[:, 0 : 2 * lon_size, lanes] = north.reshape(shape).astype(jnp.bfloat16)
        data_ref[:, 2 * lon_size : 4 * lon_size, lanes] = south.reshape(shape).astype(jnp.bfloat16)


def legendre_kernel(tiles, level, sizes, has_before, limit_ref, moved_ref, table_ref, *refs):
    out_ref, held, staged, slot_of, tile_of, last_of, in_sems, out_sems, *scratch = refs[1 if has_before else 0 :]
    data_ref = scratch[0]
    incoming = pltpu.make_async_copy(moved_ref, scratch[2] if sizes else data_ref, scratch[-1])
    incoming.start()
    buffers, stages = held.shape[0], staged.shape[0]
    levels = staged.shape[2]
    half = 2 * levels
    begin, end = 0, table_ref.shape[0]

    def tile_count(slot):
        return lax.div(limit_ref[slot] + (KTILE - 1), KTILE)

    def fetch(slot, count):
        place = lax.rem(slot, buffers)
        rows = pl.ds(0, count * KTILE)
        return pltpu.make_async_copy(table_ref.at[slot, rows, :], held.at[place, rows, :], in_sems.at[place])

    def put(slot):
        place = lax.rem(slot, stages)
        target = out_ref.at[slot, :, pl.ds(level, levels), :]
        return pltpu.make_async_copy(staged.at[place], target, out_sems.at[place])

    def by_count(slot, act):
        count = tile_count(slot)

        def choose(low, high):
            if low == high:
                act(fetch(slot, low))
                return
            middle = (low + high) // 2
            lax.cond(count <= middle, lambda: choose(low, middle), lambda: choose(middle + 1, high))

        choose(1, tiles)

    def start(slot, carry):
        by_count(slot, lambda copy: copy.start())
        return carry

    lax.fori_loop(begin, min(begin + buffers, end), start, 0)

    def list_slot(slot, total):
        def list_tile(tile, carry):
            slot_of[total + tile] = slot
            tile_of[total + tile] = tile
            return carry

        count = tile_count(slot)
        lax.fori_loop(0, count, list_tile, 0)
        last_of[slot - begin] = total + count
        return total + count

    total = lax.fori_loop(begin, end, list_slot, 0)
    final = tile_of[total - 1]
    for i in range(GROUP):
        slot_of[total + i] = end - 1
        tile_of[total + i] = final

    incoming.wait()
    if sizes:
        arrange_here(*sizes, scratch[2], data_ref, scratch[1])

    degree = lax.broadcasted_iota(jnp.int32, (half, KTILE), 1)
    parity = (1 - 2 * (degree % 2)).astype(jnp.float32)

    def enter(slot, carry):
        by_count(slot, lambda copy: copy.wait())

        @pl.when(slot - begin >= stages)
        def _():
            put(slot - stages).wait()

        def clear(tile, carry):
            cols = pl.ds(pl.multiple_of(tile * KTILE, KTILE), KTILE)
            staged[lax.rem(slot, stages), :, :, cols] = jnp.zeros((2, levels, KTILE), jnp.float32)
            return carry

        lax.fori_loop(tile_count(slot), tiles, clear, 0)
        return carry

    def leave(slot, carry):
        put(slot).start()
        return carry

    def one_tile(item):
        slot, tile = slot_of[item], tile_of[item]
        place, stage = lax.rem(slot, buffers), lax.rem(slot, stages)
        cols = pl.ds(pl.multiple_of(tile * KTILE, KTILE), KTILE)
        product = lax.dot_general(
            data_ref[slot],
            held[place, cols, :],
            (((1,), (1,)), ((), ())),
            preferred_element_type=jnp.float32,
        )
        both = product[:half] + parity * product[half:]
        both = jnp.where(degree < limit_ref[slot] - tile * KTILE, both, 0.0)
        for c in range(2):
            staged[stage, c, :, cols] = both[c * levels : (c + 1) * levels]

    def one_group(group, carry):
        fetched, entered, left = carry
        item = group * GROUP
        newest = slot_of[item + GROUP - 1]
        wanted = jnp.minimum(slot_of[item] + buffers, end)
        lax.fori_loop(fetched, wanted, start, 0)
        lax.fori_loop(entered, newest + 1, enter, 0)
        for i in range(GROUP):
            one_tile(item + i)
        done = jnp.where(last_of[newest - begin] <= item + GROUP, newest + 1, newest)
        lax.fori_loop(left, done, leave, 0)
        return jnp.maximum(fetched, wanted), newest + 1, done

    groups = lax.div(total + GROUP - 1, GROUP)
    lax.fori_loop(0, groups, one_group, (min(begin + buffers, end), begin, begin))
    for slot in range(max(begin, end - stages), end):
        put(slot).wait()


def legendre_sum(limits, moved, table, level, levels, total_levels, lat_size, lon_size, before):
    slots, degrees, lats = table.shape
    tiles = degrees // KTILE
    anywhere = pl.BlockSpec(memory_space=pl.ANY)
    here = moved.shape[2] == LANES and levels == 8
    if not here:
        moved = arrange(moved, slots, lat_size, lon_size)
    operands = [limits, moved, table] + ([] if before is None else [before])
    items = slots * tiles + GROUP
    data = [pltpu.VMEM((slots, 4 * levels, lats), jnp.bfloat16)]
    if here:
        data.append(pltpu.VMEM((lat_size, slots * 2 * levels, LANES), jnp.float32))
        data.append(pltpu.VMEM(moved.shape, jnp.bfloat16))
    return pl.pallas_call(
        functools.partial(
            legendre_kernel, tiles, level, (lat_size, lon_size) if here else None, before is not None
        ),
        out_shape=jax.ShapeDtypeStruct((slots, 2, total_levels, degrees), jnp.float32),
        in_specs=[pl.BlockSpec(memory_space=pltpu.SMEM)] + [anywhere] * (2 if before is None else 3),
        out_specs=anywhere,
        scratch_shapes=[
            pltpu.VMEM((BUFFERS, degrees, lats), jnp.bfloat16),
            pltpu.VMEM((GROUP, 2, levels, degrees), jnp.float32),
            pltpu.SMEM((items,), jnp.int32),
            pltpu.SMEM((items,), jnp.int32),
            pltpu.SMEM((slots,), jnp.int32),
            pltpu.SemaphoreType.DMA((BUFFERS,)),
            pltpu.SemaphoreType.DMA((GROUP,)),
        ]
        + data
        + [pltpu.SemaphoreType.DMA],
        input_output_aliases={} if before is None else {3: 0},
        compiler_params=pltpu.CompilerParams(vmem_limit_bytes=VMEM),
        cost_estimate=pl.CostEstimate(
            flops=slots * degrees * lats * 4 * levels,
            bytes_accessed=slots * degrees * (lats + 8 * levels),
            transcendentals=0,
        ),
        name="legendre_sum",
    )(*operands)


def after(value, earlier):
    return value if earlier is None else lax.optimization_barrier((value, earlier))[0]


def spread(vorticity, chunk, lon_size, hop_order):
    hemis, lats, part = vorticity.shape[1:]
    me = lax.axis_index("lon")

    def piece(distance, source):
        level = chunk * lon_size + (me ^ distance)
        block = lax.dynamic_index_in_dim(source, level, 0, keepdims=False) * PRESCALE
        return block.astype(jnp.float16).reshape(hemis * lats, part)

    got, source, rounded = {}, vorticity, None
    for turn, distance in enumerate(hop_order):
        if turn == 1:
            source = after(source, rounded)
        rounded = piece(distance, source)
        got[distance] = lax.ppermute(rounded, "lon", [(i, i ^ distance) for i in range(lon_size)])
    got[0] = piece(0, source)
    return got


def spread_whole(vorticity, chunk, lon_size, earlier):
    hemis, lats, part = vorticity.shape[1:]
    block = vorticity[chunk * lon_size : (chunk + 1) * lon_size] * PRESCALE
    block = after(block.astype(jnp.float16).reshape(lon_size, hemis * lats, part), earlier)
    return lax.all_to_all(block, "lon", split_axis=0, concat_axis=0, tiled=True)


def on_device(lat_size, lon_size, high, low, vorticity, legendre, wave_order):
    levels, hemis, lats, part = vorticity.shape
    slot_count = legendre.shape[0]
    devices = lat_size * lon_size
    waves = wave_order.astype(jnp.int32)
    lower, upper = waves % FIRST, waves // FIRST
    near = lower < HALF
    index = jnp.where(near, lower, FIRST - lower) * ROWS_K + jnp.where(near, 0, 2 * KEEP) + 2 * upper
    first_slot = lax.axis_index(("lat", "lon")) * slot_count
    limits = waves.shape[0] - lax.dynamic_slice_in_dim(waves, first_slot, slot_count)
    me = lax.axis_index("lon").reshape(1)
    chunks = levels // lon_size
    hop_order = sorted(range(1, lon_size), key=lambda d: (d & 1, -(d >> 1)))

    got = spread(vorticity, 0, lon_size, hop_order)
    circles = [jnp.stack([got[i].astype(jnp.float32) for i in range(lon_size)])]
    for chunk in range(1, chunks):
        circles.append(spread_whole(vorticity, chunk, lon_size, tuple(got[d] for d in hop_order)).astype(jnp.float32))
    done = None
    moved = []
    for chunk in range(chunks):
        origin = me if chunk == 0 else jnp.zeros_like(me)
        chosen = fourier_slots(after(circles[chunk], done), origin, index, high, low)
        done = chosen
        chosen = chosen.reshape(devices, slot_count * 2, hemis * lats)
        moved.append(lax.all_to_all(chosen, ("lat", "lon"), split_axis=0, concat_axis=0, tiled=True))
    result = None
    for chunk in range(chunks):
        first = chunk * lon_size
        result = legendre_sum(limits, moved[chunk], legendre, first, lon_size, levels, lat_size, lon_size, result)
    return result


def solution(mesh):
    lat_size, lon_size = mesh.shape["lat"], mesh.shape["lon"]

    def whole(vorticity, legendre, wave_order):
        high, low = second_tables(vorticity.shape[3])
        body = functools.partial(on_device, lat_size, lon_size, high, low)
        return jax.shard_map(
            body,
            mesh=mesh,
            in_specs=(P(None, None, "lat", "lon"), P(("lat", "lon"), None, None), P()),
            out_specs=P(("lat", "lon"), None, None, None),
            check_vma=False,
        )(vorticity, legendre, wave_order)

    return whole
```
